512 devices in a mesh: section: 32 (over x_hi, z, core), peer: 16 (over x_lo, y).
Axes of the slice: x: 4 (x_hi: 2, x_lo: 2; x = x_hi * 2 + x_lo), y: 8, z: 8, core: 2. Of those that a mesh axis runs over, the one named last changes fastest.
Arguments:
- section_inputs: bfloat16 [32, 16, 8, 16, 2560], P('section', 'peer'), may hold values from -6 to 6
- returned: bfloat16 [32, 16, 8, 16, 2560], P('section', 'peer'), may hold values from -6 to 6
- norm_gain: float32 [32, 2560], P('section'), may hold values from 0.25 to 1.75
- proj_in: float32 [32, 2560, 384], P('section', 'peer'), may hold values from -5 to 5
- proj_out: float32 [32, 384, 2560], P('section', 'peer'), may hold values from -5 to 5
- wiring: int32 [32, 16, 8], replicated, may hold values from -1 to 15, as said below
- active: int32 [32], replicated, may hold values from 12 to 16, as said below
Outputs:
- next_inputs: bfloat16 [32, 16, 8, 16, 2560], P('section', 'peer')
- back_grads: bfloat16 [32, 16, 8, 16, 2560], P('section', 'peer')
- proj_in_new: float32 [32, 2560, 384], P('section', 'peer')
- proj_out_new: float32 [32, 384, 2560], P('section', 'peer')
The draws below stay inside these ranges and needn't reach their ends.
Inputs may be any that keep to these rules, and one draw needn't show every extreme that they name: wiring[s, p, i] is the peer of the next section (of section 0 for the last section) that receives the micro-batch in slot i of peer p of section s, or -1 where the slot is empty. The occupied slots of a peer come first; peers at or above active[s] have none; peer q of section s has as many occupied slots as the previous section (the last one for section 0) names q. No peer receives more than 1 micro-batches from one peer, and some peer receives exactly that many from one peer. Peers 0 to active[s] - 1 of section s take part.
All inputs are finite; a program needn't handle non-finite values.
Results may differ from the reference program's by a relative error of at most 0.009.
Values may be sent and summed in bfloat16 or wider, within the bound.
No kernel may reach another device: no remote copies, remote signals or barrier semaphores. Data moves between devices by JAX's collectives and lax.ppermute only.
A program may use at most 64 MiB of HBM per device.

```python
import math
import jax
import jax.numpy as jnp
from jax import lax

D = 2560
R = 384
CAP = 8
MT = 16
N_SECTION = 32
N_PEER = 16


def wiring_tables(key):
    keys = jax.random.split(key, 5)
    min_peers = N_PEER - N_PEER // 4
    counts = jax.random.randint(keys[0], (N_SECTION,), min_peers, N_PEER + 1)
    low_section = jax.random.randint(keys[1], (), 0, N_SECTION)
    full_section = (low_section + 1 + jax.random.randint(keys[2], (), 0, N_SECTION - 2)) % N_SECTION
    section_ids = jnp.arange(N_SECTION)
    counts = jnp.where(section_ids == low_section, min_peers, counts)
    counts = jnp.where(section_ids == (low_section + N_SECTION - 1) % N_SECTION, min_peers, counts)
    counts = jnp.where(section_ids == full_section, N_PEER, counts)
    peer_ids = jnp.arange(N_PEER)
    shuffled = jax.vmap(lambda sub_key: jax.random.permutation(sub_key, N_PEER))(jax.random.split(keys[3], N_SECTION))
    ranking = shuffled + jnp.where(peer_ids[None, :] < counts[:, None], 0, N_PEER)
    ordering = jnp.argsort(ranking, axis=1)
    offsets = jax.random.randint(keys[4], (N_SECTION,), 0, N_PEER) % counts
    total_items = min_peers * CAP
    item_ids = jnp.arange(total_items)
    position = (item_ids[None, :] + offsets[:, None]) % counts[:, None]
    receiver = jnp.take_along_axis(ordering, position, axis=1)
    loads = jnp.sum((receiver[:, :, None] == peer_ids[None, None, :]).astype(jnp.int32), axis=1)
    starts = jnp.cumsum(loads, axis=1) - loads
    slot_ids = jnp.arange(CAP)
    item_of_slot = starts[:, :, None] + slot_ids[None, None, :]
    occupied = slot_ids[None, None, :] < loads[:, :, None]
    following = jnp.roll(receiver, -1, axis=0)
    flat_items = jnp.clip(item_of_slot, 0, total_items - 1).reshape(N_SECTION, N_PEER * CAP)
    targets = jnp.take_along_axis(following, flat_items, axis=1).reshape(N_SECTION, N_PEER, CAP)
    wiring = jnp.where(occupied, targets, -1).astype(jnp.int32)
    return (counts.astype(jnp.int32), wiring)


def draw_wiring(key, part):
    counts, wiring = wiring_tables(key)
    return wiring


def draw_active(key, part):
    counts, wiring = wiring_tables(key)
    return counts


def block_levels(rng, extent, pieces, smallest, high):
    level, own = 1.0, jax.random.fold_in(rng, 6)
    for axis_at, parts in pieces:
        draws = jnp.exp(jax.random.uniform(jax.random.fold_in(own, axis_at), (parts,), jnp.float32, smallest / len(pieces), high / len(pieces)))
        level = level * jnp.repeat(draws, extent[axis_at] // parts).reshape([-1 if axis == axis_at else 1 for axis in range(len(extent))])
    return level


def scatter_about(key, extent, scale, bound, shards=(), held_as=jnp.bfloat16):
    factor_of = block_levels(key, extent, shards, -0.22, 0.18) if shards else 1.0
    array = jax.random.normal(key, extent, jnp.float32) * scale * factor_of
    return jnp.minimum(jnp.maximum(array, -bound), bound).astype(held_as)


def setup_inputs(seed: int = 0) -> dict:
    arg_keys = jax.random.split(jax.random.key(seed), 8)
    return {
        "section_inputs": scatter_about(arg_keys[0], (N_SECTION, N_PEER, CAP, MT, D), 1.0, 6.0, ((0, 32), (1, 16))),
        "returned": scatter_about(arg_keys[1], (N_SECTION, N_PEER, CAP, MT, D), 1.0, 6.0, ((0, 32), (1, 16))),
        "norm_gain": jnp.clip(1.0 + 0.15 * jax.random.normal(arg_keys[2], (N_SECTION, D), jnp.float32), 0.25, 1.75),
        "proj_in": scatter_about(arg_keys[3], (N_SECTION, D, R), 1.0, 5.0, ((0, 32), (1, 16)), jnp.float32),
        "proj_out": scatter_about(arg_keys[4], (N_SECTION, R, D), 1.0, 5.0, ((0, 32), (1, 16)), jnp.float32),
        "wiring": draw_wiring(jax.random.fold_in(arg_keys[7], 71), 0),
        "active": draw_active(jax.random.fold_in(arg_keys[7], 71), 0),
    }


LEARN_RATE = 4.0
EPS = 1e-05

def move_matrix(wiring_row):
    peer_count, slot_count = wiring_row.shape
    flattened = wiring_row.reshape(-1)
    positions = jnp.arange(peer_count * slot_count)
    earlier = (flattened[None, :] == flattened[:, None]) & (positions[None, :] < positions[:, None])
    arrival = lax.optimization_barrier(jnp.sum(earlier.astype(jnp.int32), axis=1))
    targets = jnp.arange(peer_count * slot_count)
    matches = (flattened[None, :] == (targets // slot_count)[:, None]) & (arrival[None, :] == (targets % slot_count)[:, None]) & (flattened[None, :] >= 0)
    return matches.astype(jnp.float32)

def section_pass(operands):
    inputs, returned, gain_row, proj_in, proj_out, wiring_row = operands
    in_scale = 1.0 / math.sqrt(D)
    out_scale = 1.0 / math.sqrt(R)
    token_rows = inputs.reshape(-1, D).astype(jnp.float32)
    inv_rms = lax.rsqrt(lax.optimization_barrier(jnp.mean(token_rows * token_rows, axis=1, keepdims=True)) + EPS)
    normed = (token_rows * inv_rms * gain_row[None, :]).astype(jnp.bfloat16)
    whole_in = proj_in.astype(jnp.bfloat16)
    whole_out = proj_out.astype(jnp.bfloat16)
    pre_act = jnp.dot(normed, whole_in, preferred_element_type=jnp.float32) * in_scale
    hidden = jax.nn.silu(pre_act).astype(jnp.bfloat16)
    outputs = (token_rows + jnp.dot(hidden, whole_out, preferred_element_type=jnp.float32) * out_scale).astype(jnp.bfloat16)
    live_rows = jnp.repeat((wiring_row >= 0).reshape(-1), MT)
    out_grad = jnp.where(live_rows[:, None], returned.reshape(-1, D), jnp.zeros((), jnp.bfloat16))
    hidden_grad = jnp.dot(out_grad, whole_out.T, preferred_element_type=jnp.float32) * out_scale
    sigmoid = jax.nn.sigmoid(pre_act)
    pre_grad = (hidden_grad * sigmoid * (1.0 + pre_act * (1.0 - sigmoid))).astype(jnp.bfloat16)
    norm_grad = jnp.dot(pre_grad, whole_in.T, preferred_element_type=jnp.float32) * in_scale
    scaled_grad = norm_grad * gain_row[None, :]
    in_grad = out_grad.astype(jnp.float32) + inv_rms * (scaled_grad - token_rows * inv_rms * inv_rms * lax.optimization_barrier(jnp.mean(scaled_grad * token_rows, axis=1, keepdims=True)))
    in_grad = in_grad.astype(jnp.bfloat16)
    normed_peer = normed.reshape(N_PEER, CAP * MT, D).astype(jnp.float32)
    pre_grad_peer = pre_grad.reshape(N_PEER, CAP * MT, R).astype(jnp.float32)
    hidden_peer = hidden.reshape(N_PEER, CAP * MT, R).astype(jnp.float32)
    out_grad_peer = out_grad.reshape(N_PEER, CAP * MT, D).astype(jnp.float32)
    term_in = (jnp.einsum('ptd,ptr->pdr', normed_peer, pre_grad_peer) * in_scale).astype(jnp.bfloat16)
    term_out = (jnp.einsum('ptr,ptd->prd', hidden_peer, out_grad_peer) * out_scale).astype(jnp.bfloat16)
    term_in, term_out = lax.optimization_barrier((term_in, term_out))
    sum_in = lax.optimization_barrier(jnp.sum(term_in.astype(jnp.float32), axis=0))
    sum_out = lax.optimization_barrier(jnp.sum(term_out.astype(jnp.float32), axis=0))
    return (outputs.reshape(inputs.shape), in_grad.reshape(inputs.shape), sum_in, sum_out)

def move_section(operands):
    moved_out, moved_grad, wiring_prev, wiring_here = operands
    flat_out = moved_out.reshape(N_PEER * CAP, MT * D).astype(jnp.float32)
    flat_grad = moved_grad.reshape(N_PEER * CAP, MT * D).astype(jnp.float32)
    onward = jnp.dot(move_matrix(wiring_prev), flat_out, precision=lax.Precision.HIGHEST)
    backward = jnp.dot(move_matrix(wiring_here).T, flat_grad, precision=lax.Precision.HIGHEST)
    return (onward.astype(jnp.bfloat16).reshape(moved_out.shape), backward.astype(jnp.bfloat16).reshape(moved_out.shape))

def reference(section_inputs, returned, norm_gain, proj_in, proj_out, wiring, active):
    outputs, in_grads, sum_in, sum_out = lax.map(section_pass, (section_inputs, returned, norm_gain, proj_in, proj_out, wiring))
    blank = jnp.zeros_like(outputs[:1])
    outputs_before = jnp.concatenate([blank, outputs[:-1]], axis=0)
    grads_after = jnp.concatenate([in_grads[1:], blank], axis=0)
    wiring_before = jnp.concatenate([wiring[:1], wiring[:-1]], axis=0)
    next_inputs, back_grads = lax.map(move_section, (outputs_before, grads_after, wiring_before, wiring))
    active_count = active.astype(jnp.float32)[:, None, None]
    proj_in_new = proj_in - LEARN_RATE * sum_in / active_count
    proj_out_new = proj_out - LEARN_RATE * sum_out / active_count
    return (next_inputs, back_grads, proj_in_new, proj_out_new)
```

```python
import math

import jax
import jax.numpy as jnp
from jax import lax
from jax.experimental import pallas as pl
from jax.experimental.pallas import tpu as pltpu
from jax.sharding import PartitionSpec as P

LEARN_RATE = 4.0
EPS = 1e-05
COLS = 2
LANES = 128
VMEM_LIMIT = 40 * 1024 * 1024

vmem = pl.BlockSpec(memory_space=pltpu.VMEM)
smem = pl.BlockSpec(memory_space=pltpu.SMEM)


def local_kernel(body, out_shape, in_specs, bytes_moved):
    return pl.pallas_call(
        body,
        out_shape=out_shape,
        in_specs=in_specs,
        out_specs=vmem,
        compiler_params=pltpu.CompilerParams(vmem_limit_bytes=VMEM_LIMIT),
        cost_estimate=pl.CostEstimate(flops=0, bytes_accessed=bytes_moved, transcendentals=0),
    )


def spread_slots(slot_of, slots):
    peers = slot_of.shape[0]
    rows = peers // COLS
    _, tokens, width = slots.shape
    half = width // COLS

    def body(slot_ref, slots_ref, out_ref):
        for q in range(peers):
            column, y = divmod(q, rows)
            block = slots_ref[slot_ref[q]]
            for part in range(COLS):
                out_ref[part * rows + y, column] = block[:, part * half : (part + 1) * half]

    out = jax.ShapeDtypeStruct((peers, COLS, tokens, half), slots.dtype)
    return local_kernel(body, out, [smem, vmem], 4 * peers * tokens * width)(slot_of, slots)


def collect_arrivals(source_of, valid, blocks):
    peers, _, tokens, half = blocks.shape
    slots = source_of.shape[0] // COLS

    def body(source_ref, valid_ref, blocks_ref, out_ref):
        for column in range(COLS):
            for j in range(slots):
                at = column * slots + j
                block = blocks_ref[source_ref[at], column]
                out_ref[column, j] = jnp.where(valid_ref[at] > 0, block, jnp.zeros_like(block))

    out = jax.ShapeDtypeStruct((COLS, slots, tokens, half), blocks.dtype)
    return local_kernel(body, out, [smem, smem, vmem], 4 * COLS * slots * tokens * half)(
        source_of, valid, blocks
    )


def spread_arrivals(arrival_of, blocks):
    _, slots, tokens, half = blocks.shape
    peers = arrival_of.shape[0] // COLS

    def body(arrival_ref, blocks_ref, out_ref):
        for p in range(peers):
            for column in range(COLS):
                out_ref[p, column] = blocks_ref[column, arrival_ref[p * COLS + column]]

    out = jax.ShapeDtypeStruct((peers, COLS, tokens, half), blocks.dtype)
    return local_kernel(body, out, [smem, vmem], 4 * peers * COLS * tokens * half)(
        arrival_of, blocks
    )


def collect_slots(y_of, column_of, valid, blocks):
    peers, _, tokens, half = blocks.shape
    rows = peers // COLS
    slots = y_of.shape[0]

    def body(y_ref, column_ref, valid_ref, blocks_ref, out_ref):
        for i in range(slots):
            for part in range(COLS):
                block = blocks_ref[part * rows + y_ref[i], column_ref[i]]
                out_ref[i, :, part * half : (part + 1) * half] = jnp.where(
                    valid_ref[i] > 0, block, jnp.zeros_like(block)
                )

    out = jax.ShapeDtypeStruct((slots, tokens, COLS * half), blocks.dtype)
    return local_kernel(body, out, [smem, smem, smem, vmem], 8 * slots * tokens * half)(
        y_of, column_of, valid, blocks
    )


def pack_terms(term_in, term_out, rows):
    in_rows, inner = term_in.shape[0] // rows, term_in.shape[1]
    out_rows, half = term_out.shape[0] // (rows * COLS), term_out.shape[1]
    in_size = in_rows * inner // LANES
    out_size = COLS * out_rows * half // LANES

    def body(in_ref, out_term_ref, packed_ref):
        for y in range(rows):
            for c in range(inner // LANES):
                packed_ref[y, c * in_rows : (c + 1) * in_rows] = in_ref[
                    y * in_rows : (y + 1) * in_rows, c * LANES : (c + 1) * LANES
                ].astype(jnp.bfloat16)
            for c in range(half // LANES):
                both = [
                    out_term_ref[
                        (column * rows + y) * out_rows : (column * rows + y + 1) * out_rows,
                        c * LANES : (c + 1) * LANES,
                    ]
                    for column in range(COLS)
                ]
                start = in_size + c * COLS * out_rows
                packed_ref[y, start : start + COLS * out_rows] = jnp.concatenate(both).astype(
                    jnp.bfloat16
                )

    out = jax.ShapeDtypeStruct((rows, in_size + out_size, LANES), jnp.bfloat16)
    return local_kernel(body, out, [vmem, vmem], 8 * term_in.size + 8 * term_out.size)(
        term_in, term_out
    )


def unpack_columns(packed, row_count):
    return jnp.concatenate(
        [packed[at : at + row_count] for at in range(0, packed.shape[0], row_count)], axis=1
    )


def local(section_inputs, returned, norm_gain, proj_in, proj_out, wiring, active):
    sections = lax.axis_size("section")
    peers = lax.axis_size("peer")
    rows = peers // COLS
    section_now = lax.axis_index("section")
    own_peer = lax.axis_index("peer")
    column = own_peer // rows
    y = own_peer % rows
    first = column == 0
    _, _, slot_count, tokens_each, model_width = section_inputs.shape
    inner_width = proj_in.shape[2]
    half = model_width // COLS
    tokens = slot_count * tokens_each
    in_rows, out_rows = proj_in.shape[1], proj_out.shape[1]
    in_scale = 1.0 / math.sqrt(model_width)
    out_scale = 1.0 / math.sqrt(inner_width)

    def along_y(block, distance):
        route = [(p, p // rows * rows + (p + distance) % rows) for p in range(peers)]
        return lax.ppermute(block, "peer", route)

    def across(block):
        return lax.ppermute(block, "peer", [(p, (p + rows) % peers) for p in range(peers)])

    def own_half(block):
        return jnp.where(first, block[..., :half], block[..., half:])

    def other_half(block):
        return jnp.where(first, block[..., half:], block[..., :half])

    def in_order(own, other, axis):
        return jnp.where(
            first, jnp.concatenate([own, other], axis), jnp.concatenate([other, own], axis)
        )

    def gather_rows(shard, place, whole):
        whole = place(whole, shard, y)
        up = down = shard
        for step in range(1, rows // 2):
            up, down = along_y(up, 1), along_y(down, -1)
            whole = place(whole, up, (y - step) % rows)
            whole = place(whole, down, (y + step) % rows)
        cut = shard.shape[0] // 2
        far = jnp.concatenate([along_y(up[:cut], 1), along_y(down[cut:], -1)])
        return place(whole, far, (y + rows // 2) % rows)

    routes = lax.dynamic_index_in_dim(wiring, section_now, 0, keepdims=False)
    own_route = lax.dynamic_index_in_dim(routes, own_peer, 0, keepdims=False)
    live = own_route >= 0
    peer_ids = jnp.arange(peers)
    slot_ids = jnp.arange(slot_count)
    slot_of = jnp.sum(
        jnp.where(own_route[None, :] == peer_ids[:, None], slot_ids[None, :], 0), axis=1
    ).astype(jnp.int32)
    receivers = jnp.stack([y + c * rows for c in range(COLS)])
    sends = jnp.any(routes[:, :, None] == receivers[None, None, :], axis=1)
    arrival = jnp.sum(
        (sends[None] & (peer_ids[None, :] < peer_ids[:, None])[:, :, None]).astype(jnp.int32),
        axis=1,
    )
    hits = (sends.T[:, None, :]) & (arrival.T[:, None, :] == slot_ids[None, :, None])
    source_of = jnp.sum(jnp.where(hits, peer_ids[None, None, :], 0), axis=2).reshape(-1)
    source_of = source_of.astype(jnp.int32)
    arrived_any = jnp.any(hits, axis=2).reshape(-1).astype(jnp.int32)
    arrival_of = jnp.clip(arrival, 0, slot_count - 1).reshape(-1).astype(jnp.int32)
    routed = jnp.maximum(own_route, 0)

    win = proj_in[0].astype(jnp.bfloat16)
    wout = proj_out[0].astype(jnp.bfloat16)
    wout_pair = in_order(own_half(wout), across(other_half(wout)), 0)
    wout_pair = wout_pair.reshape(COLS * out_rows, half)
    whole_in = gather_rows(
        win,
        lambda whole, block, at: lax.dynamic_update_slice(whole, block, (at * in_rows, 0)),
        jnp.zeros((half, inner_width), jnp.bfloat16),
    )

    def place_out(whole, block, at):
        return lax.dynamic_update_slice(
            whole, block.reshape(COLS, 1, out_rows, half), (0, at, 0, 0)
        )

    whole_out = gather_rows(
        wout_pair, place_out, jnp.zeros((COLS, rows, out_rows, half), jnp.bfloat16)
    ).reshape(inner_width, half)

    slots = section_inputs[0, 0]
    token_rows = slots.reshape(tokens, model_width)
    out_grad = jnp.where(
        jnp.repeat(live, tokens_each)[:, None],
        returned.reshape(tokens, model_width),
        jnp.zeros((), jnp.bfloat16),
    )
    both = jnp.concatenate([other_half(token_rows), other_half(out_grad)])
    from_other = across(both)
    token_half = in_order(own_half(token_rows), from_other[:tokens], 0).astype(jnp.float32)
    grad_half = in_order(own_half(out_grad), from_other[tokens:], 0)
    wide = token_rows.astype(jnp.float32)
    own_inv = lax.rsqrt(jnp.mean(wide * wide, axis=1, keepdims=True) + EPS)
    inv_rms = in_order(own_inv, across(own_inv), 0)
    gain = own_half(norm_gain[0])[None, :]
    normed = (token_half * inv_rms * gain).astype(jnp.bfloat16)

    pre_part = jnp.dot(normed, whole_in, preferred_element_type=jnp.float32)
    hidden_part = lax.dot_general(
        grad_half, whole_out, (((1,), (1,)), ((), ())), preferred_element_type=jnp.float32
    )
    parts = jnp.concatenate([pre_part, hidden_part], axis=1)
    message = parts.astype(jnp.bfloat16)
    sums = parts + across(message).astype(jnp.float32)
    pre_act = sums[:, :inner_width] * in_scale
    hidden_grad = sums[:, inner_width:] * out_scale
    sigmoid = jax.nn.sigmoid(pre_act)
    hidden = (pre_act * sigmoid).astype(jnp.bfloat16)
    pre_grad = (hidden_grad * sigmoid * (1.0 + pre_act * (1.0 - sigmoid))).astype(jnp.bfloat16)

    term_out = (
        lax.dot_general(
            hidden, grad_half, (((0,), (0,)), ((), ())), preferred_element_type=jnp.float32
        )
        * out_scale
    )
    term_in = (
        lax.dot_general(
            normed, pre_grad, (((0,), (0,)), ((), ())), preferred_element_type=jnp.float32
        )
        * in_scale
    )
    packed = pack_terms(term_in, term_out, rows)
    groups = [[c * rows + r for r in range(rows)] for c in range(COLS)]
    summed = lax.psum_scatter(
        packed, "peer", scatter_dimension=0, tiled=True, axis_index_groups=groups
    )[0]
    in_size = in_rows * inner_width // LANES
    sum_in = unpack_columns(summed[:in_size], in_rows).astype(jnp.float32)
    pair_out = unpack_columns(summed[in_size:], COLS * out_rows)
    own_out = jnp.where(first, pair_out[:out_rows], pair_out[out_rows:])
    other_out = jnp.where(first, pair_out[out_rows:], pair_out[:out_rows])
    sum_out = in_order(own_out, across(other_out), 1).astype(jnp.float32)

    norm_grad = (
        lax.dot_general(
            pre_grad, whole_in, (((1,), (1,)), ((), ())), preferred_element_type=jnp.float32
        )
        * in_scale
    )
    along = (
        jnp.sum(pre_grad.astype(jnp.float32) * pre_act, axis=1, keepdims=True) / model_width
    )
    in_grad = (
        grad_half.astype(jnp.float32)
        + inv_rms * (norm_grad * gain - token_half * inv_rms * along)
    ).astype(jnp.bfloat16)
    behind = [(s + 1, s) for s in range(sections - 1)]
    in_grad = lax.ppermute(in_grad, "section", behind)
    in_grad = in_grad.reshape(COLS, slot_count, tokens_each, half)
    back_blocks = lax.all_to_all(
        spread_arrivals(arrival_of, in_grad), "peer", split_axis=0, concat_axis=0, tiled=True
    )
    back_grads = collect_slots(
        (routed % rows).astype(jnp.int32),
        (routed // rows).astype(jnp.int32),
        live.astype(jnp.int32),
        back_blocks,
    )

    spread = spread_slots(slot_of, slots)
    spread, message = lax.optimization_barrier((spread, message))
    next_blocks = lax.all_to_all(spread, "peer", split_axis=0, concat_axis=0, tiled=True)
    moved = collect_arrivals(source_of, arrived_any, next_blocks)
    moved = moved.reshape(COLS * tokens, half).astype(jnp.float32)
    moved_pre = jnp.dot(
        (moved * gain).astype(jnp.bfloat16), whole_in, preferred_element_type=jnp.float32
    )
    square = jnp.sum(moved * moved, axis=1, keepdims=True)
    square_high = square.astype(jnp.bfloat16)
    square_low = (square - square_high.astype(jnp.float32)).astype(jnp.bfloat16)
    moved_message = jnp.concatenate(
        [
            moved_pre.astype(jnp.bfloat16),
            square_high,
            square_low,
            jnp.zeros((COLS * tokens, LANES - 2), jnp.bfloat16),
        ],
        axis=1,
    )
    moved_other = across(moved_message).astype(jnp.float32)
    square = (
        square
        + moved_other[:, inner_width : inner_width + 1]
        + moved_other[:, inner_width + 1 : inner_width + 2]
    )
    moved_inv = lax.rsqrt(square / model_width + EPS)
    moved_act = (moved_pre + moved_other[:, :inner_width]) * moved_inv * in_scale
    moved_hidden = jax.nn.silu(moved_act).astype(jnp.bfloat16)
    outputs = (
        moved + jnp.dot(moved_hidden, whole_out, preferred_element_type=jnp.float32) * out_scale
    ).astype(jnp.bfloat16)
    outputs = outputs.reshape(COLS, tokens, half)
    stays = jnp.where(first, outputs[0], outputs[1])
    crosses = jnp.where(first, outputs[1], outputs[0])
    ahead = [(s, s + 1) for s in range(sections - 1)]
    stays = lax.ppermute(stays, "section", ahead)
    crosses = lax.ppermute(
        crosses,
        ("section", "peer"),
        [(s * peers + p, t * peers + (p + rows) % peers) for s, t in ahead for p in range(peers)],
    )
    next_inputs = in_order(stays, crosses, 1)

    active_now = lax.dynamic_index_in_dim(active, section_now, 0, keepdims=False).astype(
        jnp.float32
    )
    proj_in_new = proj_in - LEARN_RATE * sum_in[None] / active_now
    proj_out_new = proj_out - LEARN_RATE * sum_out[None] / active_now
    return (
        next_inputs.reshape(section_inputs.shape),
        back_grads.reshape(section_inputs.shape),
        proj_in_new,
        proj_out_new,
    )


def solution(mesh):
    return jax.shard_map(
        local,
        mesh=mesh,
        in_specs=(
            P("section", "peer", None, None, None),
            P("section", "peer", None, None, None),
            P("section", None),
            P("section", "peer", None),
            P("section", "peer", None),
            P(),
            P(),
        ),
        out_specs=(
            P("section", "peer", None, None, None),
            P("section", "peer", None, None, None),
            P("section", "peer", None),
            P("section", "peer", None),
        ),
        check_vma=False,
    )
```

```python
import math

import jax
import jax.numpy as jnp
from jax import lax
from jax.experimental import pallas as pl
from jax.experimental.pallas import tpu as pltpu
from jax.sharding import PartitionSpec as P

LEARN_RATE = 4.0
EPS = 1e-05
COLS = 2
LANES = 128
BACK_PIECES = 1
VMEM_LIMIT = 40 * 1024 * 1024

vmem = pl.BlockSpec(memory_space=pltpu.VMEM)
smem = pl.BlockSpec(memory_space=pltpu.SMEM)


def local_kernel(body, out_shape, in_specs, bytes_moved, out_specs=vmem):
    return pl.pallas_call(
        body,
        out_shape=out_shape,
        in_specs=in_specs,
        out_specs=out_specs,
        compiler_params=pltpu.CompilerParams(vmem_limit_bytes=VMEM_LIMIT),
        cost_estimate=pl.CostEstimate(flops=0, bytes_accessed=bytes_moved, transcendentals=0),
    )


def spread_slots(slot_of, slots):
    peers = slot_of.shape[0]
    rows = peers // COLS
    _, tokens, width = slots.shape
    half = width // COLS

    def body(slot_ref, slots_ref, out_ref):
        for q in range(peers):
            column, y = divmod(q, rows)
            block = slots_ref[slot_ref[q]]
            for part in range(COLS):
                out_ref[part * rows + y, column] = block[:, part * half : (part + 1) * half]

    out = jax.ShapeDtypeStruct((peers, COLS, tokens, half), slots.dtype)
    return local_kernel(body, out, [smem, vmem], 4 * peers * tokens * width)(slot_of, slots)


def collect_arrivals(source_of, valid, blocks):
    peers, _, tokens, half = blocks.shape
    slots = source_of.shape[0] // COLS

    def body(source_ref, valid_ref, blocks_ref, out_ref):
        for column in range(COLS):
            for j in range(slots):
                at = column * slots + j
                block = blocks_ref[source_ref[at], column]
                out_ref[column, j] = jnp.where(valid_ref[at] > 0, block, jnp.zeros_like(block))

    out = jax.ShapeDtypeStruct((COLS, slots, tokens, half), blocks.dtype)
    return local_kernel(body, out, [smem, smem, vmem], 4 * COLS * slots * tokens * half)(
        source_of, valid, blocks
    )


def spread_arrivals(arrival_of, blocks, pieces):
    _, slots, tokens, half = blocks.shape
    peers = arrival_of.shape[0] // COLS
    size = half // pieces

    def body(arrival_ref, blocks_ref, *out_refs):
        for p in range(peers):
            for column in range(COLS):
                block = blocks_ref[column, arrival_ref[p * COLS + column]]
                for k in range(pieces):
                    out_refs[k][p, column] = block[:, k * size : (k + 1) * size]

    out = [jax.ShapeDtypeStruct((peers, COLS, tokens, size), blocks.dtype)] * pieces
    return local_kernel(
        body, out, [smem, vmem], 4 * peers * COLS * tokens * half, [vmem] * pieces
    )(arrival_of, blocks)


def collect_slots(y_of, column_of, valid, pieces):
    peers, _, tokens, size = pieces[0].shape
    rows = peers // COLS
    slots = y_of.shape[0]
    half = size * len(pieces)

    def body(y_ref, column_ref, valid_ref, *refs):
        *piece_refs, out_ref = refs
        for i in range(slots):
            for part in range(COLS):
                for k, piece_ref in enumerate(piece_refs):
                    block = piece_ref[part * rows + y_ref[i], column_ref[i]]
                    start = part * half + k * size
                    out_ref[i, :, start : start + size] = jnp.where(
                        valid_ref[i] > 0, block, jnp.zeros_like(block)
                    )

    out = jax.ShapeDtypeStruct((slots, tokens, COLS * half), pieces[0].dtype)
    specs = [smem] * 3 + [vmem] * len(pieces)
    return local_kernel(body, out, specs, 8 * slots * tokens * half)(
        y_of, column_of, valid, *pieces
    )


def other_half_and_whole(column, halved, whole):
    tokens, width = whole.shape
    half = width // COLS

    def body(column_ref, halved_ref, whole_ref, out_ref):
        for part in range(COLS):

            @pl.when(column_ref[0] == part)
            def _():
                out_ref[:, :half] = halved_ref[:, (1 - part) * half : (2 - part) * half]

        out_ref[:, half:] = whole_ref[...]

    out = jax.ShapeDtypeStruct((tokens, half + width), whole.dtype)
    return local_kernel(body, out, [smem, vmem, vmem], 6 * tokens * width)(column, halved, whole)


def pack_rows(in_part, out_part, groups):
    in_rows, inner = in_part.shape[0] // groups, in_part.shape[1]
    out_rows, width = out_part.shape[0] // groups, out_part.shape[1]
    in_size = in_rows * inner // LANES
    out_size = out_rows * width // LANES

    def body(in_ref, out_part_ref, packed_ref):
        for g in range(groups):
            for c in range(inner // LANES):
                block = in_ref[g * in_rows : (g + 1) * in_rows, c * LANES : (c + 1) * LANES]
                packed_ref[g, c * in_rows : (c + 1) * in_rows] = block.astype(jnp.bfloat16)
            for c in range(0, width // LANES, 2):
                block = out_part_ref[
                    g * out_rows : (g + 1) * out_rows, c * LANES : (c + 2) * LANES
                ]
                both = jnp.concatenate([block[:, :LANES], block[:, LANES:]])
                start = in_size + c * out_rows
                packed_ref[g, start : start + 2 * out_rows] = both.astype(jnp.bfloat16)

    out = jax.ShapeDtypeStruct((groups, in_size + out_size, LANES), jnp.bfloat16)
    return local_kernel(body, out, [vmem, vmem], 8 * in_part.size + 8 * out_part.size)(
        in_part, out_part
    )


def unpack_rows(packed, in_rows, inner, out_rows, width):
    groups = packed.shape[0]
    in_size = in_rows * inner // LANES

    def body(packed_ref, in_ref, out_ref):
        for g in range(groups):
            for c in range(inner // LANES):
                in_ref[g * in_rows : (g + 1) * in_rows, c * LANES : (c + 1) * LANES] = packed_ref[
                    g, c * in_rows : (c + 1) * in_rows
                ]
        for g in range(0, groups, 2):
            for c in range(0, width // LANES, 2):
                start = in_size + c * out_rows
                pair = [
                    packed_ref[g + k, start : start + 2 * out_rows].astype(jnp.float32)
                    for k in range(2)
                ]
                for k in range(2):
                    both = [block[k * out_rows : (k + 1) * out_rows] for block in pair]
                    out_ref[
                        g * out_rows : (g + 2) * out_rows, (c + k) * LANES : (c + k + 1) * LANES
                    ] = jnp.concatenate(both).astype(jnp.bfloat16)

    out = (
        jax.ShapeDtypeStruct((groups * in_rows, inner), jnp.bfloat16),
        jax.ShapeDtypeStruct((groups * out_rows, width), jnp.bfloat16),
    )
    return local_kernel(body, out, [vmem], 4 * packed.size, (vmem, vmem))(packed)


def step_weights(scale, parts, proj_in, proj_out):
    in_rows, inner = proj_in.shape
    out_rows, width = proj_out.shape
    in_size = in_rows * inner // LANES

    def body(scale_ref, *refs):
        *part_refs, in_ref, out_part_ref, new_in_ref, new_out_ref = refs

        def total(start, size):
            blocks = [ref[start : start + size].astype(jnp.float32) for ref in part_refs]
            return sum(blocks[1:], blocks[0]) * scale_ref[0]

        for c in range(inner // LANES):
            lanes = slice(c * LANES, (c + 1) * LANES)
            new_in_ref[:, lanes] = in_ref[:, lanes] - total(c * in_rows, in_rows)
        for c in range(0, width // LANES, 2):
            both = total(in_size + c * out_rows, 2 * out_rows)
            for k in range(2):
                lanes = slice((c + k) * LANES, (c + k + 1) * LANES)
                new_out_ref[:, lanes] = (
                    out_part_ref[:, lanes] - both[k * out_rows : (k + 1) * out_rows]
                )

    out = (
        jax.ShapeDtypeStruct(proj_in.shape, jnp.float32),
        jax.ShapeDtypeStruct(proj_out.shape, jnp.float32),
    )
    specs = [smem] + [vmem] * (len(parts) + 2)
    return local_kernel(body, out, specs, 10 * proj_in.size + 10 * proj_out.size, (vmem, vmem))(
        scale, *parts, proj_in, proj_out
    )


def local(section_inputs, returned, norm_gain, proj_in, proj_out, wiring, active):
    sections = lax.axis_size("section")
    peers = lax.axis_size("peer")
    rows = peers // COLS
    section_now = lax.axis_index("section")
    own_peer = lax.axis_index("peer")
    column = own_peer // rows
    y = own_peer % rows
    first = column == 0
    _, _, slot_count, tokens_each, model_width = section_inputs.shape
    inner_width = proj_in.shape[2]
    half = model_width // COLS
    tokens = slot_count * tokens_each
    in_rows, out_rows = proj_in.shape[1], proj_out.shape[1]
    in_scale = 1.0 / math.sqrt(model_width)
    out_scale = 1.0 / math.sqrt(inner_width)

    def along_y(block, distance):
        route = [(p, p // rows * rows + (p + distance) % rows) for p in range(peers)]
        return lax.ppermute(block, "peer", route)

    def across(block):
        return lax.ppermute(block, "peer", [(p, (p + rows) % peers) for p in range(peers)])

    def own_half(block):
        return jnp.where(first, block[..., :half], block[..., half:])

    def other_half(block):
        return jnp.where(first, block[..., half:], block[..., :half])

    def in_order(own, other, axis):
        return jnp.where(
            first, jnp.concatenate([own, other], axis), jnp.concatenate([other, own], axis)
        )

    def gather_along_y(shard):
        whole = jnp.zeros((rows,) + shard.shape, shard.dtype)

        def place(whole, block, at):
            return lax.dynamic_update_slice(whole, block[None], (at % rows, 0, 0))

        whole = place(whole, shard, y)
        up = down = shard
        for step in range(1, rows // 2):
            up, down = along_y(up, 1), along_y(down, -1)
            whole = place(whole, up, y + rows - step)
            whole = place(whole, down, y + step)
        cut = shard.shape[0] // 2
        far = jnp.concatenate([along_y(up[:cut], 1), along_y(down[cut:], -1)])
        return place(whole, far, y + rows // 2)

    routes = lax.dynamic_index_in_dim(wiring, section_now, 0, keepdims=False)
    own_route = lax.dynamic_index_in_dim(routes, own_peer, 0, keepdims=False)
    live = own_route >= 0
    peer_ids = jnp.arange(peers)
    slot_ids = jnp.arange(slot_count)
    slot_of = jnp.max(
        jnp.where(own_route[None, :] == peer_ids[:, None], slot_ids[None, :], 0), axis=1
    ).astype(jnp.int32)
    receivers = jnp.stack([y + c * rows for c in range(COLS)])
    sends = jnp.any(routes[:, :, None] == receivers[None, None, :], axis=1)
    arrival = jnp.sum(
        (sends[None] & (peer_ids[None, :] < peer_ids[:, None])[:, :, None]).astype(jnp.int32),
        axis=1,
    )
    hits = (sends.T[:, None, :]) & (arrival.T[:, None, :] == slot_ids[None, :, None])
    source_of = jnp.max(jnp.where(hits, peer_ids[None, None, :], 0), axis=2).reshape(-1)
    source_of = source_of.astype(jnp.int32)
    arrived_any = jnp.any(hits, axis=2).reshape(-1).astype(jnp.int32)
    arrival_of = jnp.clip(arrival, 0, slot_count - 1).reshape(-1).astype(jnp.int32)
    routed = jnp.maximum(own_route, 0)

    slots = section_inputs[0, 0]
    token_rows = slots.reshape(tokens, model_width)
    grad_rows = returned.reshape(tokens, model_width)
    from_other = across(
        other_half_and_whole(column.reshape(1).astype(jnp.int32), token_rows, grad_rows)
    )

    wide = token_rows.astype(jnp.float32)
    own_inv = lax.rsqrt(jnp.mean(wide * wide, axis=1, keepdims=True) + EPS)
    other_inv = across(own_inv)

    gathered = gather_along_y(pack_rows(proj_in[0], proj_out[0], 1)[0])
    gathered, from_other, other_inv = lax.optimization_barrier((gathered, from_other, other_inv))
    whole_in, some_out = unpack_rows(gathered, in_rows, inner_width, out_rows, model_width)

    token_half = in_order(own_half(token_rows), from_other[:, :half], 0).astype(jnp.float32)
    pair_live = jnp.stack([routes[y + c * rows] >= 0 for c in range(COLS)]).reshape(-1)
    grad_whole = jnp.where(
        jnp.repeat(pair_live, tokens_each)[:, None],
        in_order(grad_rows, from_other[:, half:], 0),
        jnp.zeros((), jnp.bfloat16),
    )
    gain = own_half(norm_gain[0])[None, :]

    inner_half = inner_width // COLS

    inv_rms = in_order(own_inv, other_inv, 0)
    normed = (token_half * inv_rms * gain).astype(jnp.bfloat16)
    pre_part = jnp.dot(normed, whole_in, preferred_element_type=jnp.float32)
    hidden_part = lax.dot_general(
        grad_whole, some_out, (((1,), (1,)), ((), ())), preferred_element_type=jnp.float32
    )
    message = jnp.concatenate([pre_part, hidden_part], axis=1).astype(jnp.bfloat16)
    received = across(message).astype(jnp.float32)
    pre_act = (pre_part + received[:, :inner_width]) * in_scale
    hidden_other = received[:, inner_width : inner_width + inner_half]
    hidden_grad = in_order(hidden_part, hidden_other, 1) * out_scale
    sigmoid = jax.nn.sigmoid(pre_act)
    hidden = (pre_act * sigmoid).astype(jnp.bfloat16)
    pre_grad = (hidden_grad * sigmoid * (1.0 + pre_act * (1.0 - sigmoid))).astype(jnp.bfloat16)
    grad_half = own_half(grad_whole)

    some_hidden = jnp.where(first, hidden[:, :inner_half], hidden[:, inner_half:])
    term_out = (
        lax.dot_general(
            some_hidden, grad_whole, (((0,), (0,)), ((), ())), preferred_element_type=jnp.float32
        )
        * out_scale
    )
    term_in = (
        lax.dot_general(
            normed, pre_grad, (((0,), (0,)), ((), ())), preferred_element_type=jnp.float32
        )
        * in_scale
    )
    packed = pack_rows(term_in, term_out, rows)

    norm_grad = (
        lax.dot_general(
            pre_grad, whole_in, (((1,), (1,)), ((), ())), preferred_element_type=jnp.float32
        )
        * in_scale
    )
    along = (
        jnp.sum(pre_grad.astype(jnp.float32) * pre_act, axis=1, keepdims=True) / model_width
    )
    in_grad = (
        grad_half.astype(jnp.float32)
        + inv_rms * (norm_grad * gain - token_half * inv_rms * along)
    ).astype(jnp.bfloat16)
    packed, in_grad = lax.optimization_barrier((packed, in_grad))
    in_grad = lax.ppermute(in_grad, "section", [(s + 1, s) for s in range(sections - 1)])
    in_grad = in_grad.reshape(COLS, slot_count, tokens_each, half)
    spread_back = spread_arrivals(arrival_of, in_grad, BACK_PIECES)
    back_blocks = [
        lax.all_to_all(piece, "peer", split_axis=0, concat_axis=0, tiled=True)
        for piece in spread_back
    ]

    groups = [[c * rows + r for r in range(rows)] for c in range(COLS)]
    summed = lax.psum_scatter(
        packed, "peer", scatter_dimension=0, tiled=True, axis_index_groups=groups
    )[0]
    active_now = lax.dynamic_index_in_dim(active, section_now, 0, keepdims=True)
    scale = LEARN_RATE / active_now.astype(jnp.float32)
    proj_in_new, proj_out_new = step_weights(
        scale, (summed,), proj_in[0], proj_out[0]
    )
    back_grads = collect_slots(
        (routed % rows).astype(jnp.int32),
        (routed // rows).astype(jnp.int32),
        live.astype(jnp.int32),
        back_blocks,
    )

    def with_squares(sums, rows_half, width):
        square = jnp.sum(rows_half * rows_half, axis=1, keepdims=True)
        high = square.astype(jnp.bfloat16)
        low = (square - high.astype(jnp.float32)).astype(jnp.bfloat16)
        spare = jnp.zeros((high.shape[0], -(width + 2) % LANES), jnp.bfloat16)
        parts = [part.astype(jnp.bfloat16) for part in sums] + [high, low, spare]
        return square, jnp.concatenate(parts, axis=1)

    def inverse_rms(square, received, at):
        square = square + received[:, at : at + 1] + received[:, at + 1 : at + 2]
        return lax.rsqrt(square / model_width + EPS)

    spread = spread_slots(slot_of, slots)
    spread, message = lax.optimization_barrier((spread, message))
    next_blocks = lax.all_to_all(spread, "peer", split_axis=0, concat_axis=0, tiled=True)
    moved = collect_arrivals(source_of, arrived_any, next_blocks)
    moved = moved.reshape(COLS * tokens, half).astype(jnp.float32)
    moved_pre = jnp.dot(
        (moved * gain).astype(jnp.bfloat16), whole_in, preferred_element_type=jnp.float32
    )
    moved_square, moved_message = with_squares((moved_pre,), moved, inner_width)
    moved_other = across(moved_message).astype(jnp.float32)
    moved_inv = inverse_rms(moved_square, moved_other, inner_width)
    moved_act = (moved_pre + moved_other[:, :inner_width]) * moved_inv * in_scale
    moved_hidden = jax.nn.silu(moved_act).astype(jnp.bfloat16)
    whole_out = in_order(own_half(some_out), across(other_half(some_out)), 0)
    outputs = (
        moved + jnp.dot(moved_hidden, whole_out, preferred_element_type=jnp.float32) * out_scale
    ).astype(jnp.bfloat16)
    outputs = outputs.reshape(COLS, tokens, half)
    stays = jnp.where(first, outputs[0], outputs[1])
    crosses = jnp.where(first, outputs[1], outputs[0])
    ahead = [(s, s + 1) for s in range(sections - 1)]
    stays = lax.ppermute(stays, "section", ahead)
    crosses = lax.ppermute(
        crosses,
        ("section", "peer"),
        [(s * peers + p, t * peers + (p + rows) % peers) for s, t in ahead for p in range(peers)],
    )
    next_inputs = in_order(stays, crosses, 1)

    return (
        next_inputs.reshape(section_inputs.shape),
        back_grads.reshape(section_inputs.shape),
        proj_in_new[None],
        proj_out_new[None],
    )


def solution(mesh):
    return jax.shard_map(
        local,
        mesh=mesh,
        in_specs=(
            P("section", "peer", None, None, None),
            P("section", "peer", None, None, None),
            P("section", None),
            P("section", "peer", None),
            P("section", "peer", None),
            P(),
            P(),
        ),
        out_specs=(
            P("section", "peer", None, None, None),
            P("section", "peer", None, None, None),
            P("section", "peer", None),
            P("section", "peer", None),
        ),
        check_vma=False,
    )
```
